256 devices in a mesh: wide: 64 (over z, x, core), narrow: 4 (over y).
Axes of the slice: x: 4, y: 4, z: 8, core: 2. Of those that a mesh axis runs over, the one named last changes fastest.
Arguments:
- panel: bfloat16 [196608, 3, 2048], P('wide', None, 'narrow'), may hold values from -0.013671875 to 0.013671875
- tail_samples: bfloat16 [196608, 256], P('wide'), may hold values from -6 to 6
- noise: float32 [3, 2048, 256], P(None, 'narrow'), may hold values from -6 to 6
- inner: float32 [3, 2048, 2048], P(None, 'wide', 'narrow'), may hold values from -0.125 to 0.125
- diag_inverse: float32 [3, 2048, 2048], P(None, 'narrow', 'wide'), as said below
Outputs:
- samples: float32 [3, 2048, 256], P(None, 'wide')
The draws below stay inside these ranges and needn't reach their ends.
Inputs may be any that keep to these rules, and one draw needn't show every extreme that they name: `diag_inverse`: each block is lower triangular with its diagonal between 0.5 and 1.5.
All inputs are finite; a program needn't handle non-finite values.
Results may differ from the reference program's by a relative error of at most 0.0003.
Values sent between devices are 32-bit elements; how exact they have to be, the bound alone decides.
A program may use at most 64 MiB of HBM per device.

```python
import jax
import jax.numpy as jnp
from jax import lax

B = 2048
S = 256
TAIL = 196608


def draw_diag_inverse(key, part):
    key = jax.random.fold_in(key, 7)
    key_off, key_diag = jax.random.split(key)
    off = jax.random.truncated_normal(key_off, -4.0, 4.0, (3, B, B), jnp.float32) * 0.45 / jnp.sqrt(jnp.float32(B))
    diag = jax.random.uniform(key_diag, (3, B), jnp.float32, 0.5, 1.5)
    rows = lax.broadcasted_iota(jnp.int32, (3, B, B), 1)
    cols = lax.broadcasted_iota(jnp.int32, (3, B, B), 2)
    lower = jnp.where(rows > cols, off, 0.0)
    return lower + jnp.where(rows == cols, diag[:, :, None], 0.0)


def block_levels(stream_key, dims, cuts, least, high):
    loudness = 1.0
    for dim, parts in cuts:
        steps = jax.random.uniform(jax.random.fold_in(jax.random.fold_in(stream_key, 6), dim), (parts,), jnp.float32, least / len(cuts), high / len(cuts))
        loudness = loudness * jnp.repeat(jnp.exp(steps), dims[dim] // parts).reshape((-1,) + (1,) * (len(dims) - 1 - dim))
    return loudness


def gaussian(key, dims, width, most, cuts=(), kind=jnp.bfloat16):
    result = jax.random.normal(key, dims, jnp.float32) * width
    if len(cuts) > 0:
        result = block_levels(key, dims, cuts, -0.22, 0.18) * result
    return jnp.clip(result, min=-most, max=most).astype(kind)


def setup_inputs(seed: int = 0) -> dict:
    seeds = jax.random.split(jax.random.key(seed), 6)
    panel = gaussian(seeds[0], (TAIL, 3, B), TAIL ** -0.5, 0.013671875, ((0, 64), (2, 4)))
    tail_samples = gaussian(seeds[1], (TAIL, S), 1.0, 6.0, ((0, 64),))
    noise = gaussian(seeds[2], (3, B, S), 1.0, 6.0, ((1, 4),), jnp.float32)
    inner = gaussian(seeds[3], (3, B, B), B ** -0.5, 0.125, ((1, 64), (2, 4)), jnp.float32)
    diag_inverse = draw_diag_inverse(jax.random.fold_in(seeds[5], 71), 0)
    return dict(panel=panel, tail_samples=tail_samples, noise=noise, inner=inner, diag_inverse=diag_inverse)


HI = lax.Precision.HIGHEST


def reference(panel, tail_samples, noise, inner, diag_inverse):
    tail_terms = jnp.einsum("rkj,rs->kjs", panel.astype(jnp.float32), tail_samples.astype(jnp.float32), precision=HI)
    remain = noise - tail_terms
    x_two = jnp.dot(diag_inverse[2].T, remain[2], precision=HI)
    r_one = remain[1] - jnp.dot(inner[2].T, x_two, precision=HI)
    x_one = jnp.dot(diag_inverse[1].T, r_one, precision=HI)
    r_zero = remain[0] - jnp.dot(inner[1].T, x_two, precision=HI) - jnp.dot(inner[0].T, x_one, precision=HI)
    x_zero = jnp.dot(diag_inverse[0].T, r_zero, precision=HI)
    return jnp.stack([x_zero, x_one, x_two], axis=0)
```

```python
import jax
import jax.numpy as jnp
from jax import lax
from jax.experimental import pallas as pl
from jax.experimental.pallas import tpu as pltpu
from jax.sharding import PartitionSpec as P

MESH = pl.DeviceIdType.MESH
NZ, NX, NY, NC = 8, 4, 4, 2
ROWS, DEPTH, COLS, S, PIECE = 3072, 1024, 512, 256, 32
PART = 128
GROUP = S // (NZ * NC)
F32, BF16 = jnp.float32, jnp.bfloat16
D2, L21, D1, L20, L10, D0 = range(6)
SOURCE = (("d", 2), ("i", 2), ("d", 1), ("i", 1), ("i", 0), ("d", 0))
PLAN = {
    "start": [(m, 0) for m in range(6)],
    "x2": [(D2, 1), (L21, 1)],
    "tails": [(D2, 2), (D1, 1)],
    "z2": [(L21, 2), (D2, 3)],
    "g2": [(D2, 4), (L21, 3), (D1, 2), (L20, 1), (D2, 5), (D2, 6)],
    "y2": [(L21, 4), (D1, 3), (L20, 2), (L10, 1), (L21, 5), (L21, 6)],
    "u1": [(D1, 4), (L20, 3), (L10, 2), (D0, 1), (D1, 5), (D1, 6)],
    "y1": [(L20, 4), (L10, 3), (D0, 2), (L20, 5), (L10, 4), (D0, 3), (L10, 5), (L20, 6), (L10, 6)],
    "u0": [(D0, 4), (D0, 5), (D0, 6)],
}


def halves(a):
    high = a.astype(BF16)
    return high, (a - high.astype(F32)).astype(BF16)


def kernel(
    panel, tail, noise, inner, diag, out,
    pan_v, ts_v, ts_t, noise_v, noise_t, part_t, half_in, half_sum, x_in, z_sum, z_in, right, grid, high, low,
    y_buf, u_buf, solved, out_in, flat,
    load_sem, own_sem, hs, hr, xs, xr, zs, zr, gs, gr, cs, cr, rs, rr, ss, sr, ys, yr, us, ur, os, orr, ps, pr,
):
    wide, y = lax.axis_index("wide"), lax.axis_index("narrow")
    z, x, c = wide // (NX * NC), (wide // NC) % NX, wide % NC
    way = 1 - 2 * c

    def at(z_to, x_to, c_to, y_to):
        return ((z_to * NX + x_to) * NC + c_to, y_to)

    def send(src, dst, send_sem, recv_sem, to):
        return pltpu.make_async_remote_copy(
            src_ref=src, dst_ref=dst, send_sem=send_sem, recv_sem=recv_sem, device_id=to, device_id_type=MESH
        )

    def zp(k):
        return (z + k + 2 * NZ) % NZ

    def xp(k):
        return (x + k + NX) % NX

    def yp(k):
        return (y + k + NY) % NY

    mate = at(z, x, 1 - c, y)
    partners = (
        [mate]
        + [at(zp(k), x, c, y) for k in range(1, NZ)]
        + [at(z, xp(k), c, y) for k in range(1, NX)]
        + [at(z, x, c, yp(k)) for k in range(1, NY)]
    )
    barrier = pltpu.get_barrier_semaphore()
    for to in partners:
        pl.semaphore_signal(barrier, inc=1, device_id=to, device_id_type=MESH)

    chunks = ROWS // DEPTH
    loads = {}
    count = 0
    for q in range(chunks):
        rows = pl.ds(q * DEPTH, DEPTH)
        for name, src, dst in (("ts", tail.at[rows], ts_v.at[rows]), ("p2", panel.at[2, rows], pan_v.at[2, rows])):
            loads[name, q] = pltpu.make_async_copy(src, dst, load_sem.at[count])
            loads[name, q].start()
            count += 1
    own = []
    for m, (kind, k) in enumerate(SOURCE):
        src = diag.at[k] if kind == "d" else inner.at[k]
        own.append(pltpu.make_async_copy(src, grid.at[m, z, c], own_sem.at[m]))
        own[-1].start()
    for k in (1, 0):
        for q in range(chunks):
            rows = pl.ds(q * DEPTH, DEPTH)
            loads[f"p{k}", q] = pltpu.make_async_copy(panel.at[k, rows], pan_v.at[k, rows], load_sem.at[count])
            loads[f"p{k}", q].start()
            count += 1
    loads["noise"] = pltpu.make_async_copy(
        noise.at[:, pl.ds(pl.multiple_of(x * PART, PART), PART), pl.ds(pl.multiple_of(c * PART, PART), PART)],
        noise_v, load_sem.at[count])
    loads["noise"].start()

    def multiply(k):
        for q in range(chunks):
            rows = pl.ds(q * DEPTH, DEPTH)
            if k == 2:
                loads["ts", q].wait()
                ts_t[:, q * DEPTH : (q + 1) * DEPTH] = ts_v[rows, :].T
            loads[f"p{k}", q].wait()
            term = jnp.dot(ts_t[:, q * DEPTH : (q + 1) * DEPTH], pan_v[k, rows, :], preferred_element_type=F32)
            if q == 0:
                part_t[k] = term
            else:
                part_t[k] += term

    def half_send(k):
        return send(part_t.at[k, pl.ds(pl.multiple_of((1 - c) * PART, PART), PART)], half_in.at[k], hs.at[k], hr.at[k], mate)

    def x_send(k, d):
        return send(half_sum.at[k, xp(d)], x_in.at[k, x], xs.at[k, d - 1], xr.at[k, d - 1], at(z, xp(d), c, y))

    def z_send(k, d):
        return send(z_sum.at[k, zp(d)], z_in.at[k, z], zs.at[k, d - 1], zr.at[k, d - 1], at(zp(d), x, c, y))

    def g_send(k, d):
        return send(right.at[k, x], right.at[k, x], gs.at[k, d - 1], gr.at[k, d - 1], at(z, xp(d), c, y))

    def half_to_x(k):
        half_send(k).wait_recv()
        both = part_t[k, pl.ds(pl.multiple_of(c * PART, PART), PART), :] + half_in[k]
        for i in range(NX):
            half_sum[k, i] = both[:, i * PART : (i + 1) * PART]
        for d in (2, 1, 3):
            x_send(k, d).start()

    def x_to_z(k):
        for d in (1, 3, 2):
            x_send(k, d).wait_recv()
        total = half_sum[k, x]
        for d in range(1, NX):
            total = total + x_in[k, xp(d)]
        z_sum[k] = total.reshape(NZ, GROUP, PART)
        for d in (4, 3, 5, 2, 6, 1, 7):
            z_send(k, d).start()

    def z_to_g(k):
        for d in range(1, NZ):
            z_send(k, d).wait_recv()
        total = z_sum[k, z]
        for d in range(1, NZ):
            total = total + z_in[k, zp(d)]
        right[k, x] = noise_t[k, z] - total
        for d in (2, 1, 3):
            g_send(k, d).start()

    def gathered(k):
        for d in (1, 3, 2):
            g_send(k, d).wait_recv()
        return jnp.concatenate([right[k, i] for i in range(NX)], axis=1)

    def c_send(m):
        return send(grid.at[m, z, c], grid.at[m, z, c], cs.at[m], cr.at[m], mate)

    def ring(m, s):
        if s < 4:
            piece = grid.at[m, zp(-(s - 1) * way)]
        else:
            piece = grid.at[m, zp(-3 * way), c]
        return send(piece, piece, rs.at[m, s - 1], rr.at[m, s - 1], at(zp(way), x, c, y))

    def share(m, s):
        piece = grid.at[m, zp(-s * way)] if s < 4 else grid.at[m, zp(-4 * way), c]
        return send(piece, piece, ss.at[m, s - 1], sr.at[m, s - 1], mate)

    def step(m, s):
        if s == 0:
            own[m].wait()
            c_send(m).start()
        elif s == 1:
            c_send(m).wait_recv()
            ring(m, 1).start()
        elif s < 5:
            ring(m, s - 1).wait_recv()
            ring(m, s).start()
            share(m, s - 1).start()
        elif s == 5:
            ring(m, 4).wait_recv()
            share(m, 4).start()
        else:
            for q in range(1, 5):
                share(m, q).wait_recv()
            for q in range(2):
                zs_ = slice(q * NZ // 2, (q + 1) * NZ // 2)
                rows = slice(q * COLS // 2, (q + 1) * COLS // 2)
                high[m, rows], low[m, rows] = halves(grid[m, zs_].reshape(COLS // 2, COLS))

    def pump(point):
        for m, s in PLAN[point]:
            step(m, s)

    def product(m, vector):
        dims = (((1,), (1,)), ((), ())) if SOURCE[m][0] == "d" else (((1,), (0,)), ((), ()))
        v_high, v_low = halves(vector)
        both = lax.dot_general(jnp.concatenate([v_high, v_low], axis=0), high[m], dims, preferred_element_type=F32)
        rest = lax.dot_general(v_high, low[m], dims, preferred_element_type=F32)
        return both[:GROUP] + both[GROUP:] + rest

    def y_send(k, d):
        return send(y_buf.at[k, y], y_buf.at[k, y], ys.at[k, d - 1], yr.at[k, d - 1], at(z, x, c, yp(d)))

    def y_start(k, term):
        y_buf[k, y] = term
        for d in (2, 1, 3):
            y_send(k, d).start()

    def y_end(k):
        for d in (1, 3, 2):
            y_send(k, d).wait_recv()
        total = (y_buf[k, 0] + y_buf[k, 1]) + (y_buf[k, 2] + y_buf[k, 3])
        return total

    def u_send(k, d):
        return send(u_buf.at[k, x], u_buf.at[k, x], us.at[k, d - 1], ur.at[k, d - 1], at(z, xp(d), c, y))

    def u_start(k, term):
        u_buf[k, x] = term
        for d in (2, 1, 3):
            u_send(k, d).start()

    def u_end(k):
        for d in (1, 3, 2):
            u_send(k, d).wait_recv()
        return (u_buf[k, 0] + u_buf[k, 1]) + (u_buf[k, 2] + u_buf[k, 3])

    def out_send(k, d):
        return send(
            solved.at[k, zp(d) // 2], out_in.at[k, c, z], os.at[k, d - 1], orr.at[k, d - 1], at(zp(d), x, c, y)
        )

    def out_share(k):
        return send(out_in.at[k, c], out_in.at[k, c], ps.at[k], pr.at[k], mate)

    def out_start(k, vector):
        for i in range(NX):
            solved[k, i] = vector[:, i * PART : (i + 1) * PART]
        for d in (4, 3, 5, 2, 6, 1, 7):
            out_send(k, d).start()
        out_in[k, c, z] = solved[k, z // 2]

    def out_pass(k):
        for d in range(1, NZ):
            out_send(k, d).wait_recv()
        out_share(k).start()

    def out_end(k):
        out_share(k).wait_recv()
        flat[...] = out_in[k].reshape(S, PART).T
        out[k] = flat[pl.ds(pl.multiple_of(((z * NC + c) % 4) * PIECE, PIECE), PIECE), :]

    multiply(2)
    pl.semaphore_wait(barrier, len(partners))
    half_send(2).start()
    pump("start")
    multiply(1)
    half_to_x(2)
    half_send(1).start()
    pump("x2")
    multiply(0)
    half_send(0).start()
    half_to_x(1)
    half_to_x(0)
    loads["noise"].wait()
    for k in range(3):
        noise_t[k] = noise_v[k].T.reshape(NZ, GROUP, PART)
    pump("tails")
    x_to_z(2)
    pump("z2")
    z_to_g(2)
    x_to_z(1)
    pump("g2")
    y_start(2, product(D2, gathered(2)))
    z_to_g(1)
    x_to_z(0)
    pump("y2")
    x_two = y_end(2)
    u_start(1, product(L21, x_two))
    out_start(2, x_two)
    r_one = gathered(1)
    z_to_g(0)
    pump("u1")
    r_one = r_one - u_end(1)
    y_start(1, product(D1, r_one))
    pump("y1")
    upd = product(L20, x_two)
    r_zero = gathered(0)
    out_pass(2)
    x_one = y_end(1)
    u_start(0, upd + product(L10, x_one))
    out_start(1, x_one)
    pump("u0")
    out_end(2)
    r_zero = r_zero - u_end(0)
    y_start(0, product(D0, r_zero))
    out_pass(1)
    x_zero = y_end(0)
    out_start(0, x_zero)
    out_end(1)
    out_pass(0)
    for k in range(3):
        half_send(k).wait_send()
        out_share(k).wait_send()
        for d in range(1, NX):
            for copy in (x_send(k, d), g_send(k, d), y_send(k, d)):
                copy.wait_send()
        for d in range(1, NZ):
            z_send(k, d).wait_send()
            out_send(k, d).wait_send()
    for k in range(2):
        for d in range(1, NX):
            u_send(k, d).wait_send()
    for m in range(6):
        c_send(m).wait_send()
        for s in range(1, 5):
            ring(m, s).wait_send()
            share(m, s).wait_send()
    out_end(0)


def local(panel, tail_samples, noise, inner, diag_inverse):
    dma = pltpu.SemaphoreType.DMA
    anywhere = pl.BlockSpec(memory_space=pl.ANY)
    return pl.pallas_call(
        kernel,
        name="substitution",
        out_shape=jax.ShapeDtypeStruct((3, PIECE, S), F32),
        in_specs=[anywhere] * 5,
        out_specs=pl.BlockSpec(memory_space=pltpu.VMEM),
        scratch_shapes=[
            pltpu.VMEM((3, ROWS, COLS), BF16),
            pltpu.VMEM((ROWS, S), BF16),
            pltpu.VMEM((S, ROWS), BF16),
            pltpu.VMEM((3, PART, PART), F32),
            pltpu.VMEM((3, NZ, GROUP, PART), F32),
            pltpu.VMEM((3, S, COLS), F32),
            pltpu.VMEM((3, PART, COLS), F32),
            pltpu.VMEM((3, NX, PART, PART), F32),
            pltpu.VMEM((3, NX, PART, PART), F32),
            pltpu.VMEM((3, NZ, GROUP, PART), F32),
            pltpu.VMEM((3, NZ, GROUP, PART), F32),
            pltpu.VMEM((3, NX, GROUP, PART), F32),
            pltpu.VMEM((6, NZ, NC, PIECE, COLS), F32),
            pltpu.VMEM((6, COLS, COLS), BF16),
            pltpu.VMEM((6, COLS, COLS), BF16),
            pltpu.VMEM((3, NY, GROUP, COLS), F32),
            pltpu.VMEM((2, NX, GROUP, COLS), F32),
            pltpu.VMEM((3, 4, GROUP, PART), F32),
            pltpu.VMEM((3, NC, NZ, GROUP, PART), F32),
            pltpu.VMEM((PART, S), F32),
            dma((13,)), dma((6,)),
            dma((3,)), dma((3,)),
            dma((3, NX - 1)), dma((3, NX - 1)),
            dma((3, NZ - 1)), dma((3, NZ - 1)),
            dma((3, NX - 1)), dma((3, NX - 1)),
            dma((6,)), dma((6,)),
            dma((6, 4)), dma((6, 4)),
            dma((6, 4)), dma((6, 4)),
            dma((3, NY - 1)), dma((3, NY - 1)),
            dma((2, NX - 1)), dma((2, NX - 1)),
            dma((3, NZ - 1)), dma((3, NZ - 1)),
            dma((3,)), dma((3,)),
        ],
        compiler_params=pltpu.CompilerParams(
            collective_id=0, has_side_effects=True, vmem_limit_bytes=56 * 2**20
        ),
    )(
        jnp.transpose(panel, (1, 0, 2)),
        tail_samples,
        noise,
        inner,
        jnp.transpose(diag_inverse, (0, 2, 1)),
    )


def solution(mesh):
    placed = (
        P("wide", None, "narrow"),
        P("wide", None),
        P(None, "narrow", None),
        P(None, "wide", "narrow"),
        P(None, "narrow", "wide"),
    )
    return jax.shard_map(
        local, mesh=mesh, in_specs=placed, out_specs=P(None, "wide", None), check_vma=False
    )
```

```python
import jax
import jax.numpy as jnp
from jax import lax
from jax.experimental import pallas as pl
from jax.experimental.pallas import tpu as pltpu
from jax.sharding import PartitionSpec as P

MESH = pl.DeviceIdType.MESH
NZ, NX, NY, NC = 8, 4, 4, 2
ROWS, DEPTH, COLS, S, PIECE = 3072, 1024, 512, 256, 32
PART = 128
GROUP = S // (NZ * NC)
F32, BF16 = jnp.float32, jnp.bfloat16
D2, L21, D1, L20, L10, D0 = range(6)
SOURCE = (("d", 2), ("i", 2), ("d", 1), ("i", 1), ("i", 0), ("d", 0))
FLOW = (
    "mul 2", "enter", "half 2", "b 0 0", "b 1 0", "b 2 0", "b 3 0", "b 4 0", "b 5 0", "mul 1", "x 2", "b 0 1", "b 1 1",
    "half 1", "mul 0", "b 2 1", "half 0", "x 1", "b 3 1", "noise", "x 0", "b 0 2", "z 2", "b 1 2", "b 2 2", "z 1",
    "b 0 3", "z 0", "g 2", "b 1 3", "b 2 3", "b 0 4", "g 1", "b 3 2", "b 1 4", "b 4 1", "g 0", "b 0 5", "b 2 4",
    "b 5 1", "b 0 6", "solve 2", "b 1 5", "b 3 3", "b 4 2", "b 2 5", "b 1 6", "b 5 2", "b 2 6", "b 3 4", "update 1",
    "b 4 3", "out 2", "b 5 3", "b 3 5", "b 4 4", "b 3 6", "solve 1", "pre", "b 5 4", "b 4 5", "pass 2", "b 4 6",
    "b 5 5", "update 0", "out 1", "b 5 6", "write 2", "solve 0", "pass 1", "out 0", "write 1", "pass 0", "drain",
    "write 0",
)


def halves(a):
    high = a.astype(BF16)
    return high, (a - high.astype(F32)).astype(BF16)


def kernel(
    panel, tail, noise, inner, diag, out,
    pan_v, ts_v, ts_t, noise_v, noise_t, part_t, half_in, half_sum, x_in, z_sum, z_in, right, grid, high, low,
    y_buf, u_buf, solved, out_in, flat,
    load_sem, own_sem, hs, hr, xs, xr, zs, zr, gs, gr, cs, cr, rs, rr, ss, sr, ys, yr, us, ur, os, orr, ps, pr,
):
    wide, y = lax.axis_index("wide"), lax.axis_index("narrow")
    z, x, c = wide // (NX * NC), (wide // NC) % NX, wide % NC
    way = 1 - 2 * c

    def at(z_to, x_to, c_to, y_to):
        return ((z_to * NX + x_to) * NC + c_to, y_to)

    started, open_in = {}, {}

    class send:
        def __init__(self, src, dst, send_sem, recv_sem, to, key=None):
            self.copy = pltpu.make_async_remote_copy(
                src_ref=src, dst_ref=dst, send_sem=send_sem, recv_sem=recv_sem, device_id=to, device_id_type=MESH
            )
            self.key = key

        def start(self):
            self.copy.start()
            started[self.key] = self.copy
            open_in[self.key] = self.copy

        def wait_recv(self):
            self.copy.wait_recv()
            del open_in[self.key]

    def zp(k):
        return (z + k + 2 * NZ) % NZ

    def xp(k):
        return (x + k + NX) % NX

    def yp(k):
        return (y + k + NY) % NY

    mate = at(z, x, 1 - c, y)
    partners = (
        [mate]
        + [at(zp(k), x, c, y) for k in range(1, NZ)]
        + [at(z, xp(k), c, y) for k in range(1, NX)]
        + [at(z, x, c, yp(k)) for k in range(1, NY)]
    )
    barrier = pltpu.get_barrier_semaphore()
    for to in partners:
        pl.semaphore_signal(barrier, inc=1, device_id=to, device_id_type=MESH)

    chunks = ROWS // DEPTH
    loads = {}
    count = 0
    for q in range(chunks):
        rows = pl.ds(q * DEPTH, DEPTH)
        for name, src, dst in (("ts", tail.at[rows], ts_v.at[rows]), ("p2", panel.at[2, rows], pan_v.at[2, rows])):
            loads[name, q] = pltpu.make_async_copy(src, dst, load_sem.at[count])
            loads[name, q].start()
            count += 1
    own = []
    for m, (kind, k) in enumerate(SOURCE):
        src = diag.at[k] if kind == "d" else inner.at[k]
        own.append(pltpu.make_async_copy(src, grid.at[m, z, c], own_sem.at[m]))
        own[-1].start()
    for k in (1, 0):
        for q in range(chunks):
            rows = pl.ds(q * DEPTH, DEPTH)
            loads[f"p{k}", q] = pltpu.make_async_copy(panel.at[k, rows], pan_v.at[k, rows], load_sem.at[count])
            loads[f"p{k}", q].start()
            count += 1
    loads["noise"] = pltpu.make_async_copy(
        noise.at[:, pl.ds(pl.multiple_of(x * PART, PART), PART), pl.ds(pl.multiple_of(c * PART, PART), PART)],
        noise_v, load_sem.at[count])
    loads["noise"].start()

    def multiply(k):
        for q in range(chunks):
            rows = pl.ds(q * DEPTH, DEPTH)
            if k == 2:
                loads["ts", q].wait()
                ts_t[:, q * DEPTH : (q + 1) * DEPTH] = ts_v[rows, :].T
            loads[f"p{k}", q].wait()
            term = jnp.dot(ts_t[:, q * DEPTH : (q + 1) * DEPTH], pan_v[k, rows, :], preferred_element_type=F32)
            if q == 0:
                part_t[k] = term
            else:
                part_t[k] += term

    def half_send(k):
        return send(part_t.at[k, pl.ds(pl.multiple_of((1 - c) * PART, PART), PART)], half_in.at[k], hs.at[k], hr.at[k], mate, ("half_send", k))

    def x_send(k, d):
        return send(half_sum.at[k, xp(d)], x_in.at[k, x], xs.at[k, d - 1], xr.at[k, d - 1], at(z, xp(d), c, y), ("x_send", k, d))

    def z_send(k, d):
        return send(z_sum.at[k, zp(d)], z_in.at[k, z], zs.at[k, d - 1], zr.at[k, d - 1], at(zp(d), x, c, y), ("z_send", k, d))

    def g_send(k, d):
        return send(right.at[k, x], right.at[k, x], gs.at[k, d - 1], gr.at[k, d - 1], at(z, xp(d), c, y), ("g_send", k, d))

    def half_to_x(k):
        half_send(k).wait_recv()
        both = part_t[k, pl.ds(pl.multiple_of(c * PART, PART), PART), :] + half_in[k]
        for i in range(NX):
            half_sum[k, i] = both[:, i * PART : (i + 1) * PART]
        for d in (2, 1, 3):
            x_send(k, d).start()

    def x_to_z(k):
        for d in (1, 3, 2):
            x_send(k, d).wait_recv()
        total = half_sum[k, x]
        for d in range(1, NX):
            total = total + x_in[k, xp(d)]
        z_sum[k] = total.reshape(NZ, GROUP, PART)
        for d in (4, 3, 5, 2, 6, 1, 7):
            z_send(k, d).start()

    def z_to_g(k):
        for d in range(1, NZ):
            z_send(k, d).wait_recv()
        total = z_sum[k, z]
        for d in range(1, NZ):
            total = total + z_in[k, zp(d)]
        right[k, x] = noise_t[k, z] - total
        for d in (2, 1, 3):
            g_send(k, d).start()

    def gathered(k):
        for d in (1, 3, 2):
            g_send(k, d).wait_recv()
        return jnp.concatenate([right[k, i] for i in range(NX)], axis=1)

    def c_send(m):
        return send(grid.at[m, z, c], grid.at[m, z, c], cs.at[m], cr.at[m], mate, ("c_send", m))

    def ring(m, s):
        if s < 4:
            piece = grid.at[m, zp(-(s - 1) * way)]
        else:
            piece = grid.at[m, zp(-3 * way), c]
        return send(piece, piece, rs.at[m, s - 1], rr.at[m, s - 1], at(zp(way), x, c, y), ("ring", m, s))

    def share(m, s):
        piece = grid.at[m, zp(-s * way)] if s < 4 else grid.at[m, zp(-4 * way), c]
        return send(piece, piece, ss.at[m, s - 1], sr.at[m, s - 1], mate, ("share", m, s))

    def step(m, s):
        if s == 0:
            own[m].wait()
            c_send(m).start()
        elif s == 1:
            c_send(m).wait_recv()
            ring(m, 1).start()
        elif s < 5:
            ring(m, s - 1).wait_recv()
            ring(m, s).start()
            share(m, s - 1).start()
        elif s == 5:
            ring(m, 4).wait_recv()
            share(m, 4).start()
        else:
            for q in range(1, 5):
                share(m, q).wait_recv()
            for q in range(2):
                zs_ = slice(q * NZ // 2, (q + 1) * NZ // 2)
                rows = slice(q * COLS // 2, (q + 1) * COLS // 2)
                high[m, rows], low[m, rows] = halves(grid[m, zs_].reshape(COLS // 2, COLS))

    def product(m, vector):
        dims = (((1,), (1,)), ((), ())) if SOURCE[m][0] == "d" else (((1,), (0,)), ((), ()))
        v_high, v_low = halves(vector)
        both = lax.dot_general(jnp.concatenate([v_high, v_low], axis=0), high[m], dims, preferred_element_type=F32)
        rest = lax.dot_general(v_high, low[m], dims, preferred_element_type=F32)
        return both[:GROUP] + both[GROUP:] + rest

    def y_send(k, d):
        return send(y_buf.at[k, y], y_buf.at[k, y], ys.at[k, d - 1], yr.at[k, d - 1], at(z, x, c, yp(d)), ("y_send", k, d))

    def y_start(k, term):
        y_buf[k, y] = term
        for d in (2, 1, 3):
            y_send(k, d).start()

    def y_end(k):
        for d in (1, 3, 2):
            y_send(k, d).wait_recv()
        total = (y_buf[k, 0] + y_buf[k, 1]) + (y_buf[k, 2] + y_buf[k, 3])
        return total

    def u_send(k, d):
        return send(u_buf.at[k, x], u_buf.at[k, x], us.at[k, d - 1], ur.at[k, d - 1], at(z, xp(d), c, y), ("u_send", k, d))

    def u_start(k, term):
        u_buf[k, x] = term
        for d in (2, 1, 3):
            u_send(k, d).start()

    def u_end(k):
        for d in (1, 3, 2):
            u_send(k, d).wait_recv()
        return (u_buf[k, 0] + u_buf[k, 1]) + (u_buf[k, 2] + u_buf[k, 3])

    def out_send(k, d):
        return send(solved.at[k, zp(d) // 2], out_in.at[k, c, z], os.at[k, d - 1], orr.at[k, d - 1], at(zp(d), x, c, y), ("out_send", k, d))

    def out_share(k):
        return send(out_in.at[k, c], out_in.at[k, c], ps.at[k], pr.at[k], mate, ("out_share", k))

    def out_start(k, vector):
        for i in range(NX):
            solved[k, i] = vector[:, i * PART : (i + 1) * PART]
        for d in (4, 3, 5, 2, 6, 1, 7):
            out_send(k, d).start()
        out_in[k, c, z] = solved[k, z // 2]

    def out_pass(k):
        for d in range(1, NZ):
            out_send(k, d).wait_recv()
        out_share(k).start()

    def out_end(k):
        out_share(k).wait_recv()
        flat[...] = out_in[k].reshape(S, PART).T
        out[k] = flat[pl.ds(pl.multiple_of(((z * NC + c) % 4) * PIECE, PIECE), PIECE), :]

    kept = {}

    def enter():
        pl.semaphore_wait(barrier, len(partners))

    def noise_turn():
        loads["noise"].wait()
        for k in range(3):
            noise_t[k] = noise_v[k].T.reshape(NZ, GROUP, PART)

    def solve(k):
        value = gathered(k)
        if k < 2:
            value = value - u_end(k)
        y_start(k, product((D0, D1, D2)[k], value))

    def update(k):
        kept[k + 1] = y_end(k + 1)
        if k == 1:
            u_start(1, product(L21, kept[2]))
        else:
            u_start(0, kept["pre"] + product(L10, kept[1]))

    def pre():
        kept["pre"] = product(L20, kept[2])

    def to_out(k):
        if k == 0:
            kept[0] = y_end(0)
        out_start(k, kept[k])

    def drain():
        for copy in started.values():
            copy.wait_send()

    work = {
        "mul": multiply, "enter": enter, "half": lambda k: half_send(k).start(), "b": step, "x": half_to_x, "noise": noise_turn,
        "z": x_to_z, "g": z_to_g, "solve": solve, "update": update, "pre": pre, "out": to_out, "pass": out_pass,
        "write": out_end, "drain": drain,
    }
    for entry in FLOW:
        name, *numbers = entry.split()
        work[name](*map(int, numbers))


def local(panel, tail_samples, noise, inner, diag_inverse):
    dma = pltpu.SemaphoreType.DMA
    anywhere = pl.BlockSpec(memory_space=pl.ANY)
    return pl.pallas_call(
        kernel,
        name="substitution",
        out_shape=jax.ShapeDtypeStruct((3, PIECE, S), F32),
        in_specs=[anywhere] * 5,
        out_specs=pl.BlockSpec(memory_space=pltpu.VMEM),
        scratch_shapes=[
            pltpu.VMEM((3, ROWS, COLS), BF16),
            pltpu.VMEM((ROWS, S), BF16),
            pltpu.VMEM((S, ROWS), BF16),
            pltpu.VMEM((3, PART, PART), F32),
            pltpu.VMEM((3, NZ, GROUP, PART), F32),
            pltpu.VMEM((3, S, COLS), F32),
            pltpu.VMEM((3, PART, COLS), F32),
            pltpu.VMEM((3, NX, PART, PART), F32),
            pltpu.VMEM((3, NX, PART, PART), F32),
            pltpu.VMEM((3, NZ, GROUP, PART), F32),
            pltpu.VMEM((3, NZ, GROUP, PART), F32),
            pltpu.VMEM((3, NX, GROUP, PART), F32),
            pltpu.VMEM((6, NZ, NC, PIECE, COLS), F32),
            pltpu.VMEM((6, COLS, COLS), BF16),
            pltpu.VMEM((6, COLS, COLS), BF16),
            pltpu.VMEM((3, NY, GROUP, COLS), F32),
            pltpu.VMEM((2, NX, GROUP, COLS), F32),
            pltpu.VMEM((3, 4, GROUP, PART), F32),
            pltpu.VMEM((3, NC, NZ, GROUP, PART), F32),
            pltpu.VMEM((PART, S), F32),
            dma((13,)), dma((6,)),
            dma((3,)), dma((3,)),
            dma((3, NX - 1)), dma((3, NX - 1)),
            dma((3, NZ - 1)), dma((3, NZ - 1)),
            dma((3, NX - 1)), dma((3, NX - 1)),
            dma((6,)), dma((6,)),
            dma((6, 4)), dma((6, 4)),
            dma((6, 4)), dma((6, 4)),
            dma((3, NY - 1)), dma((3, NY - 1)),
            dma((2, NX - 1)), dma((2, NX - 1)),
            dma((3, NZ - 1)), dma((3, NZ - 1)),
            dma((3,)), dma((3,)),
        ],
        compiler_params=pltpu.CompilerParams(
            collective_id=0, has_side_effects=True, vmem_limit_bytes=56 * 2**20
        ),
    )(
        jnp.transpose(panel, (1, 0, 2)),
        tail_samples,
        noise,
        inner,
        jnp.transpose(diag_inverse, (0, 2, 1)),
    )


def solution(mesh):
    placed = (
        P("wide", None, "narrow"),
        P("wide", None),
        P(None, "narrow", None),
        P(None, "wide", "narrow"),
        P(None, "narrow", "wide"),
    )
    return jax.shard_map(
        local, mesh=mesh, in_specs=placed, out_specs=P(None, "wide", None), check_vma=False
    )
```

```python
import jax
import jax.numpy as jnp
from jax import lax
from jax.experimental import pallas as pl
from jax.experimental.pallas import tpu as pltpu
from jax.sharding import PartitionSpec as P

MESH = pl.DeviceIdType.MESH
NZ, NX, NY, NC = 8, 4, 4, 2
ROWS, DEPTH, COLS, S, PIECE = 3072, 1024, 512, 256, 32
PART = 128
GROUP = S // (NZ * NC)
F32, BF16 = jnp.float32, jnp.bfloat16
D2, L21, D1, L20, L10, D0 = range(6)
SOURCE = (("d", 2), ("i", 2), ("d", 1), ("i", 1), ("i", 0), ("d", 0))
FLOW = (
    "mul 2", "enter", "half 2", "b 0 0", "b 1 0", "b 2 0", "b 3 0", "b 4 0", "b 5 0", "mul 1", "x 2", "b 0 1", "b 1 1",
    "half 1", "mul 0", "b 2 1", "half 0", "x 1", "b 3 1", "noise", "x 0", "b 0 2", "z 2", "b 1 2", "b 2 2", "z 1",
    "b 0 3", "z 0", "g 2", "b 1 3", "b 2 3", "b 0 4", "g 1", "b 3 2", "b 4 1", "g 0", "b 1 4", "b 2 4", "b 0 5",
    "b 5 1", "b 0 6", "solve 2", "b 3 3", "b 4 2", "b 1 5", "b 2 5", "b 1 6", "b 5 2", "b 2 6", "b 3 4", "update 1",
    "b 4 3", "out 2", "b 5 3", "b 3 5", "b 3 6", "b 4 4", "solve 1", "pre", "b 5 4", "b 4 5", "pass 2", "b 4 6",
    "b 5 5", "update 0", "out 1", "b 5 6", "write 2", "solve 0", "pass 1", "out 0", "write 1", "pass 0", "drain",
    "write 0",
)


def halves(a):
    high = a.astype(BF16)
    return high, (a - high.astype(F32)).astype(BF16)


def kernel(
    panel, tail, noise, inner, diag, out,
    pan_v, ts_v, ts_t, noise_v, noise_t, part_t, half_in, half_sum, x_in, z_sum, z_in, right, grid, high, low,
    y_buf, u_buf, solved, out_in, flat,
    load_sem, own_sem, hs, hr, xs, xr, zs, zr, gs, gr, cs, cr, rs, rr, ss, sr, ys, yr, us, ur, os, orr, ps, pr,
):
    wide, y = lax.axis_index("wide"), lax.axis_index("narrow")
    z, x, c = wide // (NX * NC), (wide // NC) % NX, wide % NC
    way = 1 - 2 * c

    def at(z_to, x_to, c_to, y_to):
        return ((z_to * NX + x_to) * NC + c_to, y_to)

    started, open_in = {}, {}

    class send:
        def __init__(self, src, dst, send_sem, recv_sem, to, key=None):
            self.copy = pltpu.make_async_remote_copy(
                src_ref=src, dst_ref=dst, send_sem=send_sem, recv_sem=recv_sem, device_id=to, device_id_type=MESH
            )
            self.key = key

        def start(self):
            self.copy.start()
            started[self.key] = self.copy
            open_in[self.key] = self.copy

        def wait_recv(self):
            self.copy.wait_recv()
            del open_in[self.key]

    def zp(k):
        return (z + k + 2 * NZ) % NZ

    def xp(k):
        return (x + k + NX) % NX

    def yp(k):
        return (y + k + NY) % NY

    mate = at(z, x, 1 - c, y)
    partners = (
        [mate]
        + [at(zp(k), x, c, y) for k in range(1, NZ)]
        + [at(z, xp(k), c, y) for k in range(1, NX)]
        + [at(z, x, c, yp(k)) for k in range(1, NY)]
    )
    barrier = pltpu.get_barrier_semaphore()
    for to in partners:
        pl.semaphore_signal(barrier, inc=1, device_id=to, device_id_type=MESH)

    chunks = ROWS // DEPTH
    loads = {}
    count = 0
    for q in range(chunks):
        rows = pl.ds(q * DEPTH, DEPTH)
        for name, src, dst in (("ts", tail.at[rows], ts_v.at[rows]), ("p2", panel.at[2, rows], pan_v.at[2, rows])):
            loads[name, q] = pltpu.make_async_copy(src, dst, load_sem.at[count])
            loads[name, q].start()
            count += 1
    own = []
    for m, (kind, k) in enumerate(SOURCE):
        src = diag.at[k] if kind == "d" else inner.at[k]
        own.append(pltpu.make_async_copy(src, grid.at[m, z, c], own_sem.at[m]))
        own[-1].start()
    for k in (1, 0):
        for q in range(chunks):
            rows = pl.ds(q * DEPTH, DEPTH)
            loads[f"p{k}", q] = pltpu.make_async_copy(panel.at[k, rows], pan_v.at[k, rows], load_sem.at[count])
            loads[f"p{k}", q].start()
            count += 1
    loads["noise"] = pltpu.make_async_copy(
        noise.at[:, pl.ds(pl.multiple_of(x * PART, PART), PART), pl.ds(pl.multiple_of(c * PART, PART), PART)],
        noise_v, load_sem.at[count])
    loads["noise"].start()

    def multiply(k):
        for q in range(chunks):
            rows = pl.ds(q * DEPTH, DEPTH)
            if k == 2:
                loads["ts", q].wait()
                ts_t[:, q * DEPTH : (q + 1) * DEPTH] = ts_v[rows, :].T
            loads[f"p{k}", q].wait()
            term = jnp.dot(ts_t[:, q * DEPTH : (q + 1) * DEPTH], pan_v[k, rows, :], preferred_element_type=F32)
            if q == 0:
                part_t[k] = term
            else:
                part_t[k] += term

    def half_send(k):
        return send(part_t.at[k, pl.ds(pl.multiple_of((1 - c) * PART, PART), PART)], half_in.at[k], hs.at[k], hr.at[k], mate, ("half_send", k))

    def x_send(k, d):
        return send(half_sum.at[k, xp(d)], x_in.at[k, x], xs.at[k, d - 1], xr.at[k, d - 1], at(z, xp(d), c, y), ("x_send", k, d))

    def z_send(k, d):
        return send(z_sum.at[k, zp(d)], z_in.at[k, z], zs.at[k, d - 1], zr.at[k, d - 1], at(zp(d), x, c, y), ("z_send", k, d))

    def g_send(k, d):
        return send(right.at[k, x], right.at[k, x], gs.at[k, d - 1], gr.at[k, d - 1], at(z, xp(d), c, y), ("g_send", k, d))

    def half_to_x(k):
        half_send(k).wait_recv()
        both = part_t[k, pl.ds(pl.multiple_of(c * PART, PART), PART), :] + half_in[k]
        for i in range(NX):
            half_sum[k, i] = both[:, i * PART : (i + 1) * PART]
        for d in (2, 1, 3):
            x_send(k, d).start()

    def x_to_z(k):
        for d in (1, 3, 2):
            x_send(k, d).wait_recv()
        total = half_sum[k, x]
        for d in range(1, NX):
            total = total + x_in[k, xp(d)]
        z_sum[k] = total.reshape(NZ, GROUP, PART)
        for d in (4, 3, 5, 2, 6, 1, 7):
            z_send(k, d).start()

    def z_to_g(k):
        for d in range(1, NZ):
            z_send(k, d).wait_recv()
        total = z_sum[k, z]
        for d in range(1, NZ):
            total = total + z_in[k, zp(d)]
        right[k, x] = noise_t[k, z] - total
        for d in (2, 1, 3):
            g_send(k, d).start()

    def gathered(k):
        for d in (1, 3, 2):
            g_send(k, d).wait_recv()
        return jnp.concatenate([right[k, i] for i in range(NX)], axis=1)

    def c_send(m):
        return send(grid.at[m, z, c], grid.at[m, z, c], cs.at[m], cr.at[m], mate, ("c_send", m))

    def ring(m, s):
        if s < 4:
            piece = grid.at[m, zp(-(s - 1) * way)]
        else:
            piece = grid.at[m, zp(-3 * way), c]
        return send(piece, piece, rs.at[m, s - 1], rr.at[m, s - 1], at(zp(way), x, c, y), ("ring", m, s))

    def share(m, s):
        piece = grid.at[m, zp(-s * way)] if s < 4 else grid.at[m, zp(-4 * way), c]
        return send(piece, piece, ss.at[m, s - 1], sr.at[m, s - 1], mate, ("share", m, s))

    def step(m, s):
        if s == 0:
            own[m].wait()
            c_send(m).start()
        elif s == 1:
            c_send(m).wait_recv()
            ring(m, 1).start()
        elif s < 5:
            ring(m, s - 1).wait_recv()
            ring(m, s).start()
            share(m, s - 1).start()
        elif s == 5:
            ring(m, 4).wait_recv()
            share(m, 4).start()
        else:
            for q in range(1, 5):
                share(m, q).wait_recv()
            for q in range(2):
                zs_ = slice(q * NZ // 2, (q + 1) * NZ // 2)
                rows = slice(q * COLS // 2, (q + 1) * COLS // 2)
                high[m, rows], low[m, rows] = halves(grid[m, zs_].reshape(COLS // 2, COLS))

    def product(m, vector):
        dims = (((1,), (1,)), ((), ())) if SOURCE[m][0] == "d" else (((1,), (0,)), ((), ()))
        v_high, v_low = halves(vector)
        both = lax.dot_general(jnp.concatenate([v_high, v_low], axis=0), high[m], dims, preferred_element_type=F32)
        rest = lax.dot_general(v_high, low[m], dims, preferred_element_type=F32)
        return both[:GROUP] + both[GROUP:] + rest

    def y_send(k, d):
        return send(y_buf.at[k, y], y_buf.at[k, y], ys.at[k, d - 1], yr.at[k, d - 1], at(z, x, c, yp(d)), ("y_send", k, d))

    def y_start(k, term):
        y_buf[k, y] = term
        for d in (2, 1, 3):
            y_send(k, d).start()

    def y_end(k):
        for d in (1, 3, 2):
            y_send(k, d).wait_recv()
        total = (y_buf[k, 0] + y_buf[k, 1]) + (y_buf[k, 2] + y_buf[k, 3])
        return total

    def u_send(k, d):
        return send(u_buf.at[k, x], u_buf.at[k, x], us.at[k, d - 1], ur.at[k, d - 1], at(z, xp(d), c, y), ("u_send", k, d))

    def u_start(k, term):
        u_buf[k, x] = term
        for d in (2, 1, 3):
            u_send(k, d).start()

    def u_end(k):
        for d in (1, 3, 2):
            u_send(k, d).wait_recv()
        return (u_buf[k, 0] + u_buf[k, 1]) + (u_buf[k, 2] + u_buf[k, 3])

    def out_send(k, d):
        return send(solved.at[k, zp(d) // 2], out_in.at[k, c, z], os.at[k, d - 1], orr.at[k, d - 1], at(zp(d), x, c, y), ("out_send", k, d))

    def out_share(k):
        return send(out_in.at[k, c], out_in.at[k, c], ps.at[k], pr.at[k], mate, ("out_share", k))

    def out_start(k, vector):
        for i in range(NX):
            solved[k, i] = vector[:, i * PART : (i + 1) * PART]
        for d in (4, 3, 5, 2, 6, 1, 7):
            out_send(k, d).start()
        out_in[k, c, z] = solved[k, z // 2]

    def out_pass(k):
        for d in range(1, NZ):
            out_send(k, d).wait_recv()
        out_share(k).start()

    def out_end(k):
        out_share(k).wait_recv()
        flat[...] = out_in[k].reshape(S, PART).T
        out[k] = flat[pl.ds(pl.multiple_of(((z * NC + c) % 4) * PIECE, PIECE), PIECE), :]

    kept = {}

    def enter():
        pl.semaphore_wait(barrier, len(partners))

    def noise_turn():
        loads["noise"].wait()
        for k in range(3):
            noise_t[k] = noise_v[k].T.reshape(NZ, GROUP, PART)

    def solve(k):
        value = gathered(k)
        if k < 2:
            value = value - u_end(k)
        y_start(k, product((D0, D1, D2)[k], value))

    def update(k):
        kept[k + 1] = y_end(k + 1)
        if k == 1:
            u_start(1, product(L21, kept[2]))
        else:
            u_start(0, kept["pre"] + product(L10, kept[1]))

    def pre():
        kept["pre"] = product(L20, kept[2])

    def to_out(k):
        if k == 0:
            kept[0] = y_end(0)
        out_start(k, kept[k])

    def drain():
        for copy in started.values():
            copy.wait_send()

    work = {
        "mul": multiply, "enter": enter, "half": lambda k: half_send(k).start(), "b": step, "x": half_to_x, "noise": noise_turn,
        "z": x_to_z, "g": z_to_g, "solve": solve, "update": update, "pre": pre, "out": to_out, "pass": out_pass,
        "write": out_end, "drain": drain,
    }
    for entry in FLOW:
        name, *numbers = entry.split()
        work[name](*map(int, numbers))


def local(panel, tail_samples, noise, inner, diag_inverse):
    dma = pltpu.SemaphoreType.DMA
    anywhere = pl.BlockSpec(memory_space=pl.ANY)
    return pl.pallas_call(
        kernel,
        name="substitution",
        out_shape=jax.ShapeDtypeStruct((3, PIECE, S), F32),
        in_specs=[anywhere] * 5,
        out_specs=pl.BlockSpec(memory_space=pltpu.VMEM),
        scratch_shapes=[
            pltpu.VMEM((3, ROWS, COLS), BF16),
            pltpu.VMEM((ROWS, S), BF16),
            pltpu.VMEM((S, ROWS), BF16),
            pltpu.VMEM((3, PART, PART), F32),
            pltpu.VMEM((3, NZ, GROUP, PART), F32),
            pltpu.VMEM((3, S, COLS), F32),
            pltpu.VMEM((3, PART, COLS), F32),
            pltpu.VMEM((3, NX, PART, PART), F32),
            pltpu.VMEM((3, NX, PART, PART), F32),
            pltpu.VMEM((3, NZ, GROUP, PART), F32),
            pltpu.VMEM((3, NZ, GROUP, PART), F32),
            pltpu.VMEM((3, NX, GROUP, PART), F32),
            pltpu.VMEM((6, NZ, NC, PIECE, COLS), F32),
            pltpu.VMEM((6, COLS, COLS), BF16),
            pltpu.VMEM((6, COLS, COLS), BF16),
            pltpu.VMEM((3, NY, GROUP, COLS), F32),
            pltpu.VMEM((2, NX, GROUP, COLS), F32),
            pltpu.VMEM((3, 4, GROUP, PART), F32),
            pltpu.VMEM((3, NC, NZ, GROUP, PART), F32),
            pltpu.VMEM((PART, S), F32),
            dma((13,)), dma((6,)),
            dma((3,)), dma((3,)),
            dma((3, NX - 1)), dma((3, NX - 1)),
            dma((3, NZ - 1)), dma((3, NZ - 1)),
            dma((3, NX - 1)), dma((3, NX - 1)),
            dma((6,)), dma((6,)),
            dma((6, 4)), dma((6, 4)),
            dma((6, 4)), dma((6, 4)),
            dma((3, NY - 1)), dma((3, NY - 1)),
            dma((2, NX - 1)), dma((2, NX - 1)),
            dma((3, NZ - 1)), dma((3, NZ - 1)),
            dma((3,)), dma((3,)),
        ],
        compiler_params=pltpu.CompilerParams(
            collective_id=0, has_side_effects=True, vmem_limit_bytes=56 * 2**20
        ),
    )(
        jnp.transpose(panel, (1, 0, 2)),
        tail_samples,
        noise,
        inner,
        jnp.transpose(diag_inverse, (0, 2, 1)),
    )


def solution(mesh):
    placed = (
        P("wide", None, "narrow"),
        P("wide", None),
        P(None, "narrow", None),
        P(None, "wide", "narrow"),
        P(None, "narrow", "wide"),
    )
    return jax.shard_map(
        local, mesh=mesh, in_specs=placed, out_specs=P(None, "wide", None), check_vma=False
    )
```
